32 devices in a mesh: level: 8 (over z, x), sample: 4 (over y, core).
Axes of the slice: x: 2, y: 2, z: 4, core: 2. Of those that a mesh axis runs over, the one named last changes fastest.
Arguments:
- samples: bfloat16 [32768, 512], P('level', 'sample'), may hold values from -6 to 6
- sketch: bfloat16 [2, 128, 256], replicated, may hold values from -0.375 to 0.375
Outputs:
- far_factors: float32 [128, 128, 128], P('level')
- near_factors: float32 [64, 128, 128], P('level')
- basis_rows: float32 [8192, 512], P('level', 'sample')
The draws below stay inside these ranges and needn't reach their ends.
All inputs are finite; a program needn't handle non-finite values.
Results may differ from the reference program's by a relative error of at most 0.0031.
Values may be sent and summed in bfloat16 or wider, within the bound.
A program may use at most 64 MiB of HBM per device.

```python
import math
import jax
import jax.numpy as jnp
from jax import lax

RANK = 128
SAMPLES = 512
ROWS_DEV = 4096
ORDER = 32768
N_LEVEL = 8


def levels(key, dims, pieces, low, largest):
    def one(dim, blocks):
        draws = jax.random.uniform(jax.random.fold_in(jax.random.fold_in(key, 6), dim), (blocks,), jnp.float32, low / len(pieces), largest / len(pieces))
        return jnp.repeat(jnp.exp(draws), dims[dim] // blocks).reshape((-1,) + (1,) * (len(dims) - dim - 1))

    gain = one(*pieces[0])
    for cut in pieces[1:]:
        gain = gain * one(*cut)
    return gain


def gaussian(stream_key, extent, width, most, split=(), held_as=jnp.bfloat16):
    entries = width * jax.random.normal(stream_key, extent, jnp.float32)
    if split:
        entries = entries * levels(stream_key, extent, split, -0.22, 0.18)
    return jnp.clip(entries, -most, most).astype(held_as)


def setup_inputs(seed: int = 0) -> dict:
    arg_keys = jax.random.split(jax.random.key(seed), 3)
    samples = gaussian(arg_keys[0], (ORDER, SAMPLES), 1.0, 6.0, ((0, 8), (1, 4)))
    sketch = gaussian(arg_keys[1], (2, RANK, 2 * RANK), (2 * RANK) ** -0.5, 0.375)
    return dict(samples=samples, sketch=sketch)


def level_step(rows, sketch_level, distance):
    groups = rows.shape[0]
    half = rows.shape[1] // 2
    columns = rows.shape[2]
    index = jnp.arange(groups, dtype=jnp.int32)
    partner = rows[jnp.bitwise_xor(index, distance)]
    upper = (index // distance % 2 == 1)[:, None, None]
    lower_rows = jnp.where(upper, partner[:, half:], rows[:, :half])
    upper_rows = jnp.where(upper, rows[:, half:], partner[:, :half])
    boxes = half // RANK
    left = sketch_level[:, :RANK].astype(jnp.float32)
    right = sketch_level[:, RANK:].astype(jnp.float32)

    def one_group(pair):
        first = pair[0].reshape(boxes, RANK, columns).astype(jnp.float32)
        second = pair[1].reshape(boxes, RANK, columns).astype(jnp.float32)
        projected = jnp.einsum('rm,bmc->brc', left, first) + jnp.einsum('rm,bmc->brc', right, second)
        gram = jnp.einsum('brc,bsc->brs', projected, projected, precision=lax.Precision.HIGHEST)
        factor = jnp.linalg.cholesky(gram)

        def solve_box(factor_box, block_box):
            return jax.scipy.linalg.solve_triangular(factor_box, block_box, lower=True)
        solved = jax.vmap(solve_box)(factor, projected) * math.sqrt(SAMPLES)
        return (factor, solved.reshape(boxes * RANK, columns))
    return lax.map(one_group, (lower_rows, upper_rows))

def reference(samples, sketch):
    columns = samples.shape[1]
    rows = samples.reshape(N_LEVEL, ROWS_DEV, columns)
    far, first = level_step(rows, sketch[0], N_LEVEL // 2)
    first = first.astype(jnp.bfloat16)
    near, second = level_step(first, sketch[1], 1)
    return (far.reshape(-1, RANK, RANK), near.reshape(-1, RANK, RANK), second.reshape(-1, columns))
```

```python
import functools
import math

import jax
import jax.numpy as jnp
from jax import lax
from jax.experimental import pallas as pl
from jax.experimental.pallas import tpu as pltpu
from jax.sharding import PartitionSpec as P

SAMPLES = 512
RANK = 128
PANEL = 8
F32 = jnp.float32
BF16 = jnp.bfloat16


def split(value):
    high = value.astype(BF16).astype(F32)
    return high, value - high


def project_kernel(
    distance, group, rows_ref, sketch_ref, z_ref, gram_ref,
    arrived, part, first, partial, second, third,
    row_send, row_recv, first_send, first_recv, second_send, second_recv, third_send, third_recv,
):
    level, sample = lax.axis_index("level"), lax.axis_index("sample")
    upper = level // distance % 2
    other = level + distance - 2 * distance * upper
    core = sample % 2
    mate = sample + 1 - 2 * core
    across = sample + 2 - 4 * (sample // 2 % 2)
    count = arrived.shape[0]
    boxes = count // RANK
    chunks = boxes // group
    half = group // 2

    barrier = pltpu.get_barrier_semaphore()
    for target in ({"level": other}, {"sample": mate}, {"sample": across}):
        pl.semaphore_signal(barrier, inc=1, device_id=target, device_id_type=pl.DeviceIdType.MESH)
    pl.semaphore_wait(barrier, 3)

    def remote(src, dst, send, recv, c, target):
        return pltpu.make_async_remote_copy(
            src_ref=src, dst_ref=dst, send_sem=send.at[c], recv_sem=recv.at[c],
            device_id=target, device_id_type=pl.DeviceIdType.MESH,
        )

    size = group * RANK
    swaps = []
    for c in range(chunks):
        start = pl.multiple_of((1 - upper) * count + c * size, size)
        swap = remote(
            rows_ref.at[pl.ds(start, size)], arrived.at[pl.ds(c * size, size)],
            row_send, row_recv, c, {"level": other},
        )
        swap.start()
        swaps.append(swap)

    left = sketch_ref[:, :RANK].astype(F32)
    right = sketch_ref[:, RANK:].astype(F32)
    with_kept = jnp.where(upper == 1, right, left).astype(BF16)
    with_arrived = jnp.where(upper == 1, left, right).astype(BF16)

    firsts, seconds, thirds = [], [], []

    def compute(c):
        swaps[c].wait_recv()
        for b in range(c * group, (c + 1) * group):
            kept = rows_ref[pl.ds(pl.multiple_of(upper * count + b * RANK, RANK), RANK), :]
            z = jnp.dot(with_kept, kept, preferred_element_type=F32)
            z = z + jnp.dot(with_arrived, arrived[b * RANK:(b + 1) * RANK, :], preferred_element_type=F32)
            z_ref[b] = z
            high, low = split(z)
            high, low = high.astype(BF16), low.astype(BF16)
            part[b] = lax.dot_general(
                jnp.concatenate((high, low, high, low), axis=1),
                jnp.concatenate((high, high, low, low), axis=1),
                (((1,), (1,)), ((), ())), preferred_element_type=F32,
            )
        copy = remote(
            part.at[pl.ds(c * group + (1 - core) * half, half)], first.at[pl.ds(c * half, half)],
            first_send, first_recv, c, {"sample": mate},
        )
        copy.start()
        firsts.append(copy)

    def add_first(c):
        firsts[c].wait_recv()
        for b in range(half):
            partial[c * half + b] = part[c * group + core * half + b] + first[c * half + b]
        copy = remote(
            partial.at[pl.ds(c * half, half)], second.at[pl.ds(c * half, half)],
            second_send, second_recv, c, {"sample": across},
        )
        copy.start()
        seconds.append(copy)

    def add_second(c):
        seconds[c].wait_recv()
        for b in range(half):
            gram_ref[c * group + core * half + b] = partial[c * half + b] + second[c * half + b]
        copy = remote(
            gram_ref.at[pl.ds(c * group + core * half, half)], third.at[pl.ds(c * half, half)],
            third_send, third_recv, c, {"sample": mate},
        )
        copy.start()
        thirds.append(copy)

    def take_third(c):
        thirds[c].wait_recv()
        for b in range(half):
            gram_ref[c * group + (1 - core) * half + b] = third[c * half + b]

    stages = (compute, add_first, add_second, take_third)
    for step in range(chunks + len(stages) - 1):
        for depth, stage in enumerate(stages):
            if 0 <= step - depth < chunks:
                stage(step - depth)
    for copy in swaps + firsts + seconds + thirds:
        copy.wait_send()


def project(rows, sketch_level, distance, group, collective_id):
    count, columns = rows.shape[0] // 2, rows.shape[1]
    boxes = count // RANK
    chunks = boxes // group
    square = (RANK, RANK)
    vmem = pl.BlockSpec(memory_space=pltpu.VMEM)
    return pl.pallas_call(
        functools.partial(project_kernel, distance, group),
        out_shape=(
            jax.ShapeDtypeStruct((boxes, RANK, columns), F32),
            jax.ShapeDtypeStruct((boxes,) + square, F32),
        ),
        in_specs=[vmem, vmem],
        out_specs=(vmem, vmem),
        scratch_shapes=[
            pltpu.VMEM((count, columns), BF16),
            pltpu.VMEM((boxes,) + square, F32),
        ] + [pltpu.VMEM((boxes // 2,) + square, F32)] * 4
        + [pltpu.SemaphoreType.DMA((chunks,))] * 8,
        compiler_params=pltpu.CompilerParams(
            collective_id=collective_id, has_side_effects=True, vmem_limit_bytes=40 * 2**20
        ),
    )(rows, sketch_level)


def factor_kernel(gram_ref, z_ref, factor_ref, rows_ref, work, done):
    boxes, order, _ = gram_ref.shape
    tile = (PANEL, 128)
    lane = lax.broadcasted_iota(jnp.int32, tile, 1)
    row = lax.broadcasted_iota(jnp.int32, tile, 0)
    box_of = lane // PANEL
    unit = (lane % PANEL == row).astype(F32)
    picks = [box_of * PANEL + k for k in range(PANEL)]

    work[:, :, :order] = gram_ref[...]
    work[:, :, order:] = z_ref[...]

    def across_rows(value, j):
        return jnp.broadcast_to(value[j:j + 1, :], (PANEL, value.shape[1]))

    def panel(top, p, carry):
        start = pl.multiple_of(p * PANEL, PANEL)
        packed = unit
        for m in range(boxes):
            shift = lax.rem(m * PANEL + order - p * PANEL, order)
            moved = pltpu.roll(work[m, pl.ds(start, PANEL), :order], shift, axis=1)
            packed = jnp.where(box_of == m, moved, packed)
        column = [jnp.take_along_axis(packed, pick, axis=1) for pick in picks]
        inverse = unit
        for j in range(PANEL):
            scale = lax.rsqrt(across_rows(column[j], j))
            below = column[j] * scale
            for k in range(j + 1, PANEL):
                column[k] = column[k] - below * (across_rows(column[k], j) * scale)
            solved = across_rows(inverse, j) * scale
            inverse = jnp.where(
                row > j, inverse - below * solved, jnp.where(row == j, solved, inverse)
            )
        for m in range(boxes):
            old = work[m, pl.ds(start, PANEL), :]
            new = None
            for k in range(PANEL):
                at = m * PANEL + k
                term = jnp.broadcast_to(inverse[:, at:at + 1], old.shape) * across_rows(old, k)
                new = term if new is None else new + term
            done[m, pl.ds(start, PANEL), :] = new
            high, low = split(new)
            right = jnp.concatenate((high, high, low, low), axis=0).astype(BF16)
            left = jnp.concatenate((high, low, high, low), axis=0)[:, :order]
            left = left.T[top:, :].astype(BF16)
            work[m, top:, :] = work[m, top:, :] - jnp.dot(left, right, preferred_element_type=F32)
        return carry

    strip = 4
    for top in range(0, order // PANEL, strip):
        lax.fori_loop(top, top + strip, functools.partial(panel, top * PANEL), 0)

    keep = lax.broadcasted_iota(jnp.int32, (order, order), 0) >= lax.broadcasted_iota(
        jnp.int32, (order, order), 1
    )

    def finish(m, carry):
        factor_ref[m] = jnp.where(keep, done[m, :, :order].T, 0.0)
        rows_ref[m] = (done[m, :, order:] * math.sqrt(SAMPLES)).astype(rows_ref.dtype)
        return carry

    lax.fori_loop(0, boxes, finish, 0)


def factor(gram, z, dtype):
    boxes, order, columns = z.shape
    together = min(16, boxes)
    spec = pl.BlockSpec((together, order, order), lambda i: (i, 0, 0))
    wide = pl.BlockSpec((together, order, columns), lambda i: (i, 0, 0))
    factors, rows = pl.pallas_call(
        factor_kernel,
        grid=(boxes // together,),
        out_shape=(
            jax.ShapeDtypeStruct((boxes, order, order), F32),
            jax.ShapeDtypeStruct((boxes, order, columns), dtype),
        ),
        in_specs=[spec, wide],
        out_specs=(spec, wide),
        scratch_shapes=[pltpu.VMEM((together, order, order + columns), F32)] * 2,
        compiler_params=pltpu.CompilerParams(vmem_limit_bytes=40 * 2**20),
    )(gram, z)
    return factors, rows.reshape(boxes * order, columns)


def shards(samples, sketch):
    far = lax.axis_size("level") // 2
    z, gram = project(samples, sketch[0], far, 4, 0)
    far_factors, first_rows = factor(gram, z, BF16)
    z, gram = project(first_rows, sketch[1], 1, 2, 1)
    near_factors, basis_rows = factor(gram, z, F32)
    return (far_factors, near_factors, basis_rows)


def solution(mesh):
    return jax.shard_map(
        shards,
        mesh=mesh,
        in_specs=(P("level", "sample"), P()),
        out_specs=(P("level", None, None), P("level", None, None), P("level", "sample")),
        check_vma=False,
    )
```

```python
import functools
import math

import jax
import jax.numpy as jnp
from jax import lax
from jax.experimental import pallas as pl
from jax.experimental.pallas import tpu as pltpu
from jax.sharding import PartitionSpec as P

SAMPLES = 512
RANK = 128
PANEL = 8
F32 = jnp.float32
BF16 = jnp.bfloat16


def split(value):
    high = value.astype(BF16).astype(F32)
    return high, value - high


def project_kernel(
    distance, group, rows_ref, sketch_ref, z_ref, gram_ref,
    arrived, part, first, partial, second, third,
    row_send, row_recv, first_send, first_recv, second_send, second_recv, third_send, third_recv,
):
    level, sample = lax.axis_index("level"), lax.axis_index("sample")
    upper = level // distance % 2
    other = level + distance - 2 * distance * upper
    core = sample % 2
    mate = sample + 1 - 2 * core
    across = sample + 2 - 4 * (sample // 2 % 2)
    count = arrived.shape[0]
    boxes = count // RANK
    chunks = boxes // group
    half = group // 2

    barrier = pltpu.get_barrier_semaphore()
    for target in ({"level": other}, {"sample": mate}, {"sample": across}):
        pl.semaphore_signal(barrier, inc=1, device_id=target, device_id_type=pl.DeviceIdType.MESH)
    pl.semaphore_wait(barrier, 3)

    def remote(src, dst, send, recv, c, target):
        return pltpu.make_async_remote_copy(
            src_ref=src, dst_ref=dst, send_sem=send.at[c], recv_sem=recv.at[c],
            device_id=target, device_id_type=pl.DeviceIdType.MESH,
        )

    size = group * RANK
    swaps = []
    for c in range(chunks):
        start = pl.multiple_of((1 - upper) * count + c * size, size)
        swap = remote(
            rows_ref.at[pl.ds(start, size)], arrived.at[pl.ds(c * size, size)],
            row_send, row_recv, c, {"level": other},
        )
        swap.start()
        swaps.append(swap)

    left = sketch_ref[:, :RANK].astype(F32)
    right = sketch_ref[:, RANK:].astype(F32)
    with_kept = jnp.where(upper == 1, right, left).astype(BF16)
    with_arrived = jnp.where(upper == 1, left, right).astype(BF16)

    firsts, seconds, thirds = [], [], []

    def compute(c):
        swaps[c].wait_recv()
        for b in range(c * group, (c + 1) * group):
            kept = rows_ref[pl.ds(pl.multiple_of(upper * count + b * RANK, RANK), RANK), :]
            z = jnp.dot(with_kept, kept, preferred_element_type=F32)
            z = z + jnp.dot(with_arrived, arrived[b * RANK:(b + 1) * RANK, :], preferred_element_type=F32)
            z_ref[b] = z
            high, low = split(z)
            high, low = high.astype(BF16), low.astype(BF16)
            part[b] = lax.dot_general(
                jnp.concatenate((high, low, high, low), axis=1),
                jnp.concatenate((high, high, low, low), axis=1),
                (((1,), (1,)), ((), ())), preferred_element_type=F32,
            )
        copy = remote(
            part.at[pl.ds(c * group + (1 - core) * half, half)], first.at[pl.ds(c * half, half)],
            first_send, first_recv, c, {"sample": mate},
        )
        copy.start()
        firsts.append(copy)

    def add_first(c):
        firsts[c].wait_recv()
        for b in range(half):
            partial[c * half + b] = part[c * group + core * half + b] + first[c * half + b]
        copy = remote(
            partial.at[pl.ds(c * half, half)], second.at[pl.ds(c * half, half)],
            second_send, second_recv, c, {"sample": across},
        )
        copy.start()
        seconds.append(copy)

    def add_second(c):
        seconds[c].wait_recv()
        for b in range(half):
            gram_ref[c * group + core * half + b] = partial[c * half + b] + second[c * half + b]
        copy = remote(
            gram_ref.at[pl.ds(c * group + core * half, half)], third.at[pl.ds(c * half, half)],
            third_send, third_recv, c, {"sample": mate},
        )
        copy.start()
        thirds.append(copy)

    def take_third(c):
        thirds[c].wait_recv()
        for b in range(half):
            gram_ref[c * group + (1 - core) * half + b] = third[c * half + b]

    stages = (compute, add_first, add_second, take_third)
    for step in range(chunks + len(stages) - 1):
        for depth, stage in enumerate(stages):
            if 0 <= step - depth < chunks:
                stage(step - depth)
    for copy in swaps + firsts + seconds + thirds:
        copy.wait_send()


def project(rows, sketch_level, distance, group, collective_id):
    count, columns = rows.shape[0] // 2, rows.shape[1]
    boxes = count // RANK
    chunks = boxes // group
    square = (RANK, RANK)
    vmem = pl.BlockSpec(memory_space=pltpu.VMEM)
    return pl.pallas_call(
        functools.partial(project_kernel, distance, group),
        out_shape=(
            jax.ShapeDtypeStruct((boxes, RANK, columns), F32),
            jax.ShapeDtypeStruct((boxes,) + square, F32),
        ),
        in_specs=[vmem, vmem],
        out_specs=(vmem, vmem),
        scratch_shapes=[
            pltpu.VMEM((count, columns), BF16),
            pltpu.VMEM((boxes,) + square, F32),
        ] + [pltpu.VMEM((boxes // 2,) + square, F32)] * 4
        + [pltpu.SemaphoreType.DMA((chunks,))] * 8,
        compiler_params=pltpu.CompilerParams(
            collective_id=collective_id, has_side_effects=True, vmem_limit_bytes=40 * 2**20
        ),
    )(rows, sketch_level)


def factor_kernel(gram_ref, z_ref, factor_ref, rows_ref, work, done):
    boxes, order, _ = gram_ref.shape
    strip = 4 * PANEL
    lane = lax.broadcasted_iota(jnp.int32, (PANEL, 128), 1)
    row = lax.broadcasted_iota(jnp.int32, (PANEL, 128), 0)
    box_of = lane // PANEL
    unit = (lane % PANEL == row).astype(F32)
    zeros = jnp.zeros((PANEL, 128), F32)
    picks = [box_of * PANEL + k for k in range(PANEL)]
    tiles = range(4)

    work[:, :, :order] = gram_ref[...]
    work[:, :, order:] = z_ref[...]

    def across_rows(value, j):
        return jnp.broadcast_to(value[j:j + 1, :], value.shape)

    def turn(value, groups):
        shift = groups * PANEL % 128
        return pltpu.roll(value, shift, axis=1) if shift else value

    def strip_inverse(top):
        grid = [[unit if a == c else zeros for c in tiles] for a in tiles]
        for a in tiles:
            for m in range(boxes):
                old = work[m, top + a * PANEL:top + (a + 1) * PANEL, :order]
                for c in tiles:
                    moved = turn(old, m - top // PANEL - c)
                    grid[a][c] = jnp.where(box_of == m, moved, grid[a][c])
        for b in tiles:
            rest = range(b, 4)
            column = {
                (a, k): jnp.take_along_axis(grid[a][b], picks[k], axis=1)
                for a in rest for k in range(PANEL)
            }
            for a in rest:
                grid[a][b] = unit if a == b else zeros
            for j in range(PANEL):
                scale = lax.rsqrt(across_rows(column[b, j], j))
                below = {a: column[a, j] * scale for a in rest}
                for k in range(j + 1, PANEL):
                    solved = across_rows(column[b, k], j) * scale
                    for a in rest:
                        column[a, k] = column[a, k] - below[a] * solved
                for c in tiles:
                    solved = across_rows(grid[b][c], j) * scale
                    for a in rest:
                        new = grid[a][c] - below[a] * solved
                        if a == b:
                            new = jnp.where(row > j, new, jnp.where(row == j, solved, grid[a][c]))
                        grid[a][c] = new
        return grid

    for top in range(0, order, strip):
        grid = strip_inverse(top)
        panels = []
        for m in range(boxes):
            pieces = []
            for a in tiles:
                piece = zeros
                for c in range(a + 1):
                    piece = jnp.where(box_of == c, turn(grid[a][c], c - m), piece)
                pieces.append(piece)
            inverse = jnp.concatenate(pieces, axis=0)[:, :strip]
            high, low = split(inverse)
            left = jnp.concatenate((high, low), axis=0).astype(BF16)
            high, low = split(work[m, top:top + strip, :])
            right = jnp.concatenate((high, low), axis=1).astype(BF16)
            terms = jnp.dot(left, right, preferred_element_type=F32)
            wide = terms.shape[1] // 2
            new = terms[:strip, :wide] + (
                terms[strip:, :wide] + terms[:strip, wide:] + terms[strip:, wide:]
            )
            done[m, top:top + strip, :] = new
            panels.append(new)
        if top + strip < order:
            for m in range(boxes):
                high, low = split(panels[m])
                right = jnp.concatenate((high, high, low, low), axis=0).astype(BF16)
                left = jnp.concatenate((high, low, high, low), axis=0)[:, :order]
                left = left.T[top + strip:, :].astype(BF16)
                work[m, top + strip:, :] = work[m, top + strip:, :] - jnp.dot(
                    left, right, preferred_element_type=F32
                )

    keep = lax.broadcasted_iota(jnp.int32, (order, order), 0) >= lax.broadcasted_iota(
        jnp.int32, (order, order), 1
    )
    for m in range(boxes):
        factor_ref[m] = jnp.where(keep, done[m, :, :order].T, 0.0)
        rows_ref[m] = (done[m, :, order:] * math.sqrt(SAMPLES)).astype(rows_ref.dtype)


def factor(gram, z, dtype):
    boxes, order, columns = z.shape
    together = min(16, boxes)
    spec = pl.BlockSpec((together, order, order), lambda i: (i, 0, 0))
    wide = pl.BlockSpec((together, order, columns), lambda i: (i, 0, 0))
    factors, rows = pl.pallas_call(
        factor_kernel,
        grid=(boxes // together,),
        out_shape=(
            jax.ShapeDtypeStruct((boxes, order, order), F32),
            jax.ShapeDtypeStruct((boxes, order, columns), dtype),
        ),
        in_specs=[spec, wide],
        out_specs=(spec, wide),
        scratch_shapes=[pltpu.VMEM((together, order, order + columns), F32)] * 2,
        compiler_params=pltpu.CompilerParams(vmem_limit_bytes=40 * 2**20),
    )(gram, z)
    return factors, rows.reshape(boxes * order, columns)


def shards(samples, sketch):
    far = lax.axis_size("level") // 2
    z, gram = project(samples, sketch[0], far, 4, 0)
    far_factors, first_rows = factor(gram, z, BF16)
    z, gram = project(first_rows, sketch[1], 1, 2, 1)
    near_factors, basis_rows = factor(gram, z, F32)
    return (far_factors, near_factors, basis_rows)


def solution(mesh):
    return jax.shard_map(
        shards,
        mesh=mesh,
        in_specs=(P("level", "sample"), P()),
        out_specs=(P("level", None, None), P("level", None, None), P("level", "sample")),
        check_vma=False,
    )
```

```python
import functools
import math

import jax
import jax.numpy as jnp
from jax import lax
from jax.experimental import pallas as pl
from jax.experimental.pallas import tpu as pltpu
from jax.sharding import PartitionSpec as P

SAMPLES = 512
RANK = 128
PANEL = 8
F32 = jnp.float32
BF16 = jnp.bfloat16


def split(value):
    high = value.astype(BF16).astype(F32)
    return high, value - high


def project_kernel(
    which, distance, group, relayed, rows_ref, sketch_ref, z_ref, gram_ref,
    kept, relay, arrived, part, first, partial, second, third, kept_sem,
    own_send, row_recv, outer_recv, inner_recv, outer_pass, inner_pass,
    first_send, first_recv, second_send, second_recv, third_send, third_recv,
):
    level, sample = lax.axis_index("level"), lax.axis_index("sample")
    upper = level // distance % 2
    other = level + distance - 2 * distance * upper
    core = sample % 2
    mate = sample + 1 - 2 * core
    across = sample + 2 - 4 * (sample // 2 % 2)
    count = arrived.shape[0]
    boxes = count // RANK
    chunks = boxes // group
    half = group // 2
    size = group * RANK
    if relayed:
        hop = distance // 2
        place = level // hop % 4
        inner = (place + 1) // 2 % 2
        beside = level + hop * (1 - 2 * (place % 2))
        cross = level + hop * (3 - 2 * place)
        targets = ({"level": beside}, {"level": cross}, {"sample": mate}, {"sample": across})
    else:
        targets = ({"level": other}, {"sample": mate}, {"sample": across})

    keep = pltpu.make_async_copy(
        rows_ref.at[pl.ds(pl.multiple_of(upper * count, size), count)], kept, kept_sem
    )
    keep.start()
    barrier = pltpu.get_barrier_semaphore()
    for target in targets:
        pl.semaphore_signal(barrier, inc=1, device_id=target, device_id_type=pl.DeviceIdType.MESH)
    pl.semaphore_wait(barrier, len(targets))

    def remote(src, dst, send, recv, c, target):
        return pltpu.make_async_remote_copy(
            src_ref=src, dst_ref=dst, send_sem=send.at[c], recv_sem=recv.at[c],
            device_id=target, device_id_type=pl.DeviceIdType.MESH,
        )

    def given(c):
        return rows_ref.at[pl.ds(pl.multiple_of((1 - upper) * count + c * size, size), size)]

    def at(c):
        return pl.ds(c * size, size)

    if relayed:
        outward = [
            remote(given(c), relay.at[0, at(c)], own_send, outer_recv, c, {"level": beside})
            for c in range(chunks)
        ]
        inward = [
            remote(given(c), relay.at[1, at(c)], own_send, inner_recv, c, {"level": cross})
            for c in range(chunks)
        ]
        swaps = [
            remote(relay.at[0, at(c)], arrived.at[at(c)], outer_pass, row_recv, c, {"level": cross})
            for c in range(chunks)
        ]
        passes = [
            remote(relay.at[1, at(c)], arrived.at[at(c)], inner_pass, row_recv, c, {"level": beside})
            for c in range(chunks)
        ]

        @pl.when(inner == 0)
        def _():
            for copy in outward:
                copy.start()

        @pl.when(inner == 1)
        def _():
            for copy in inward[:2]:
                copy.start()
    else:
        swaps = [
            remote(given(c), arrived.at[at(c)], own_send, row_recv, c, {"level": other})
            for c in range(chunks)
        ]
        for copy in swaps:
            copy.start()

    left = sketch_ref[which, :, :RANK].astype(F32)
    right = sketch_ref[which, :, RANK:].astype(F32)
    with_kept = jnp.where(upper == 1, right, left).astype(BF16)
    with_arrived = jnp.where(upper == 1, left, right).astype(BF16)
    keep.wait()

    firsts, seconds, thirds = [], [], []

    def relay_on(c):
        @pl.when(inner == 1)
        def _():
            outward[c].wait_recv()
            swaps[c].start()
            if c + 2 < chunks:
                inward[c + 2].start()
            inward[c].wait_recv()
            passes[c].start()

    def compute(c):
        swaps[c].wait_recv()
        for b in range(c * group, (c + 1) * group):
            block = slice(b * RANK, (b + 1) * RANK)
            z = jnp.dot(with_kept, kept[block, :], preferred_element_type=F32)
            z = z + jnp.dot(with_arrived, arrived[block, :], preferred_element_type=F32)
            z_ref[b] = z
            high, low = split(z)
            high, low = high.astype(BF16), low.astype(BF16)
            part[b] = lax.dot_general(
                jnp.concatenate((high, low, high, low), axis=1),
                jnp.concatenate((high, high, low, low), axis=1),
                (((1,), (1,)), ((), ())), preferred_element_type=F32,
            )
        copy = remote(
            part.at[pl.ds(c * group + (1 - core) * half, half)], first.at[pl.ds(c * half, half)],
            first_send, first_recv, c, {"sample": mate},
        )
        copy.start()
        firsts.append(copy)

    def add_first(c):
        firsts[c].wait_recv()
        for b in range(half):
            partial[c * half + b] = part[c * group + core * half + b] + first[c * half + b]
        copy = remote(
            partial.at[pl.ds(c * half, half)], second.at[pl.ds(c * half, half)],
            second_send, second_recv, c, {"sample": across},
        )
        copy.start()
        seconds.append(copy)

    def add_second(c):
        seconds[c].wait_recv()
        for b in range(half):
            gram_ref[c * group + core * half + b] = partial[c * half + b] + second[c * half + b]
        copy = remote(
            gram_ref.at[pl.ds(c * group + core * half, half)], third.at[pl.ds(c * half, half)],
            third_send, third_recv, c, {"sample": mate},
        )
        copy.start()
        thirds.append(copy)

    def take_third(c):
        thirds[c].wait_recv()
        for b in range(half):
            gram_ref[c * group + (1 - core) * half + b] = third[c * half + b]

    stages = (compute, add_first, add_second, take_third)
    if relayed:
        stages = (relay_on,) + stages
    for step in range(chunks + len(stages) - 1):
        for depth, stage in enumerate(stages):
            if 0 <= step - depth < chunks:
                stage(step - depth)
    for copy in firsts + seconds + thirds:
        copy.wait_send()
    if relayed:
        for copy in outward:
            copy.wait_send()

        @pl.when(inner == 1)
        def _():
            for copy in swaps + passes:
                copy.wait_send()
    else:
        for copy in swaps:
            copy.wait_send()


def project(rows, sketch, which, distance, group, relayed):
    count, columns = rows.shape[0] // 2, rows.shape[1]
    boxes = count // RANK
    chunks = boxes // group
    square = (RANK, RANK)
    vmem = pl.BlockSpec(memory_space=pltpu.VMEM)
    half = pltpu.VMEM((boxes // 2,) + square, F32)
    return pl.pallas_call(
        functools.partial(project_kernel, which, distance, group, relayed),
        out_shape=(
            jax.ShapeDtypeStruct((boxes, RANK, columns), F32),
            jax.ShapeDtypeStruct((boxes,) + square, F32),
        ),
        in_specs=[pl.BlockSpec(memory_space=pltpu.HBM), vmem],
        out_specs=(vmem, vmem),
        scratch_shapes=[
            pltpu.VMEM((count, columns), BF16),
            pltpu.VMEM((2, count if relayed else 16, columns), BF16),
            pltpu.VMEM((count, columns), BF16),
            pltpu.VMEM((boxes,) + square, F32),
            half, half, half, half,
            pltpu.SemaphoreType.DMA,
        ] + [pltpu.SemaphoreType.DMA((chunks,))] * 12,
        compiler_params=pltpu.CompilerParams(
            collective_id=which, has_side_effects=True, vmem_limit_bytes=40 * 2**20
        ),
    )(rows, sketch)


def factor_kernel(gram_ref, z_ref, factor_ref, rows_ref, work, done):
    boxes, order, _ = gram_ref.shape
    strip = 4 * PANEL
    lane = lax.broadcasted_iota(jnp.int32, (PANEL, 128), 1)
    row = lax.broadcasted_iota(jnp.int32, (PANEL, 128), 0)
    box_of = lane // PANEL
    unit = (lane % PANEL == row).astype(F32)
    zeros = jnp.zeros((PANEL, 128), F32)
    picks = [box_of * PANEL + k for k in range(PANEL)]
    tiles = range(4)

    work[:, :, :order] = gram_ref[...]
    work[:, :, order:] = z_ref[...]

    def across_rows(value, j):
        return jnp.broadcast_to(value[j:j + 1, :], value.shape)

    def turn(value, groups):
        shift = groups * PANEL % 128
        return pltpu.roll(value, shift, axis=1) if shift else value

    def strip_inverse(top):
        grid = [[unit if a == c else zeros for c in tiles] for a in tiles]
        for a in tiles:
            for m in range(boxes):
                old = work[m, top + a * PANEL:top + (a + 1) * PANEL, :order]
                for c in tiles:
                    moved = turn(old, m - top // PANEL - c)
                    grid[a][c] = jnp.where(box_of == m, moved, grid[a][c])
        for b in tiles:
            rest = range(b, 4)
            column = {
                (a, k): jnp.take_along_axis(grid[a][b], picks[k], axis=1)
                for a in rest for k in range(PANEL)
            }
            for a in rest:
                grid[a][b] = unit if a == b else zeros
            for j in range(PANEL):
                scale = lax.rsqrt(across_rows(column[b, j], j))
                below = {a: column[a, j] * scale for a in rest}
                for k in range(j + 1, PANEL):
                    solved = across_rows(column[b, k], j) * scale
                    for a in rest:
                        column[a, k] = column[a, k] - below[a] * solved
                for c in tiles:
                    solved = across_rows(grid[b][c], j) * scale
                    for a in rest:
                        new = grid[a][c] - below[a] * solved
                        if a == b:
                            new = jnp.where(row > j, new, jnp.where(row == j, solved, grid[a][c]))
                        grid[a][c] = new
        return grid

    for top in range(0, order, strip):
        grid = strip_inverse(top)
        panels = []
        for m in range(boxes):
            pieces = []
            for a in tiles:
                piece = zeros
                for c in range(a + 1):
                    piece = jnp.where(box_of == c, turn(grid[a][c], c - m), piece)
                pieces.append(piece)
            inverse = jnp.concatenate(pieces, axis=0)[:, :strip]
            high, low = split(inverse)
            left = jnp.concatenate((high, low), axis=0).astype(BF16)
            high, low = split(work[m, top:top + strip, :])
            right = jnp.concatenate((high, low), axis=1).astype(BF16)
            terms = jnp.dot(left, right, preferred_element_type=F32)
            wide = terms.shape[1] // 2
            new = terms[:strip, :wide] + (
                terms[strip:, :wide] + terms[:strip, wide:] + terms[strip:, wide:]
            )
            done[m, top:top + strip, :] = new
            panels.append(new)
        if top + strip < order:
            for m in range(boxes):
                high, low = split(panels[m])
                right = jnp.concatenate((high, high, low, low), axis=0).astype(BF16)
                left = jnp.concatenate((high, low, high, low), axis=0)[:, :order]
                left = left.T[top + strip:, :].astype(BF16)
                work[m, top + strip:, :] = work[m, top + strip:, :] - jnp.dot(
                    left, right, preferred_element_type=F32
                )

    keep = lax.broadcasted_iota(jnp.int32, (order, order), 0) >= lax.broadcasted_iota(
        jnp.int32, (order, order), 1
    )
    for m in range(boxes):
        factor_ref[m] = jnp.where(keep, done[m, :, :order].T, 0.0)
        rows_ref[m] = (done[m, :, order:] * math.sqrt(SAMPLES)).astype(rows_ref.dtype)


def factor(gram, z, dtype):
    boxes, order, columns = z.shape
    together = min(16, boxes)
    spec = pl.BlockSpec((together, order, order), lambda i: (i, 0, 0))
    wide = pl.BlockSpec((together, order, columns), lambda i: (i, 0, 0))
    factors, rows = pl.pallas_call(
        factor_kernel,
        grid=(boxes // together,),
        out_shape=(
            jax.ShapeDtypeStruct((boxes, order, order), F32),
            jax.ShapeDtypeStruct((boxes, order, columns), dtype),
        ),
        in_specs=[spec, wide],
        out_specs=(spec, wide),
        scratch_shapes=[pltpu.VMEM((together, order, order + columns), F32)] * 2,
        compiler_params=pltpu.CompilerParams(vmem_limit_bytes=40 * 2**20),
    )(gram, z)
    return factors, rows.reshape(boxes * order, columns)


def shards(samples, sketch):
    far = lax.axis_size("level") // 2
    z, gram = project(samples, sketch, 0, far, 2, far >= 2)
    far_factors, first_rows = factor(gram, z, BF16)
    z, gram = project(first_rows, sketch, 1, 1, 2, False)
    near_factors, basis_rows = factor(gram, z, F32)
    return (far_factors, near_factors, basis_rows)


def solution(mesh):
    return jax.shard_map(
        shards,
        mesh=mesh,
        in_specs=(P("level", "sample"), P()),
        out_specs=(P("level", None, None), P("level", None, None), P("level", "sample")),
        check_vma=False,
    )
```

```python
import functools
import math

import jax
import jax.numpy as jnp
from jax import lax
from jax.experimental import pallas as pl
from jax.experimental.pallas import tpu as pltpu
from jax.sharding import PartitionSpec as P

SAMPLES = 512
RANK = 128
PANEL = 8
PACKED = 72
F32 = jnp.float32
BF16 = jnp.bfloat16


def split(value):
    high = value.astype(BF16).astype(F32)
    return high, value - high


def pack_masks():
    side = RANK // 2
    lane = lax.broadcasted_iota(jnp.int32, (side, RANK), 1)
    row = lax.broadcasted_iota(jnp.int32, (side, RANK), 0)
    return lane < side, row - lane % side


def pack(gram):
    side = RANK // 2
    first, below = pack_masks()
    top, bottom = gram[:side, :], gram[side:, :]
    main = jnp.where(first == (below >= 0), top, bottom)
    middle = jnp.where(below == 0, jnp.where(first, bottom, top), 0.0)
    middle = jnp.sum(middle, axis=0, keepdims=True)
    return jnp.concatenate((main, jnp.broadcast_to(middle, (PACKED - side, RANK))), axis=0)


def unpack(packed):
    side = RANK // 2
    first, below = pack_masks()
    main = packed[:side, :]
    middle = jnp.broadcast_to(packed[side:side + 1, :], main.shape)
    turned = jnp.concatenate((main, main), axis=0).T
    lower = jnp.where(below == 0, middle, turned[:side, :])
    upper = jnp.where(below == 0, middle, turned[side:, :])
    top = jnp.where(first, jnp.where(below >= 0, main, turned[:side, :]), jnp.where(below < 0, main, lower))
    bottom = jnp.where(first, jnp.where(below < 0, main, upper), jnp.where(below >= 0, main, turned[side:, :]))
    return jnp.concatenate((top, bottom), axis=0)


def project_kernel(
    which, distance, group, relayed, rows_ref, sketch_ref, z_ref, gram_ref,
    kept, relay, arrived, part, first, partial, second, third, kept_sem,
    own_send, row_recv, outer_recv, inner_recv, outer_pass, inner_pass,
    first_send, first_recv, second_send, second_recv, third_send, third_recv,
):
    level, sample = lax.axis_index("level"), lax.axis_index("sample")
    upper = level // distance % 2
    other = level + distance - 2 * distance * upper
    core = sample % 2
    mate = sample + 1 - 2 * core
    across = sample + 2 - 4 * (sample // 2 % 2)
    count = arrived.shape[0]
    boxes = count // RANK
    chunks = boxes // group
    half = group // 2
    size = group * RANK
    if relayed:
        hop = distance // 2
        place = level // hop % 4
        inner = (place + 1) // 2 % 2
        beside = level + hop * (1 - 2 * (place % 2))
        cross = level + hop * (3 - 2 * place)
        targets = ({"level": beside}, {"level": cross}, {"sample": mate}, {"sample": across})
    else:
        targets = ({"level": other}, {"sample": mate}, {"sample": across})

    keep = pltpu.make_async_copy(
        rows_ref.at[pl.ds(pl.multiple_of(upper * count, size), count)], kept, kept_sem
    )
    keep.start()
    barrier = pltpu.get_barrier_semaphore()
    for target in targets:
        pl.semaphore_signal(barrier, inc=1, device_id=target, device_id_type=pl.DeviceIdType.MESH)
    pl.semaphore_wait(barrier, len(targets))

    def remote(src, dst, send, recv, c, target):
        return pltpu.make_async_remote_copy(
            src_ref=src, dst_ref=dst, send_sem=send.at[c], recv_sem=recv.at[c],
            device_id=target, device_id_type=pl.DeviceIdType.MESH,
        )

    def given(c):
        return rows_ref.at[pl.ds(pl.multiple_of((1 - upper) * count + c * size, size), size)]

    def at(c):
        return pl.ds(c * size, size)

    if relayed:
        outward = [
            remote(given(c), relay.at[0, at(c)], own_send, outer_recv, c, {"level": beside})
            for c in range(chunks)
        ]
        inward = [
            remote(given(c), relay.at[1, at(c)], own_send, inner_recv, c, {"level": cross})
            for c in range(chunks)
        ]
        swaps = [
            remote(relay.at[0, at(c)], arrived.at[at(c)], outer_pass, row_recv, c, {"level": cross})
            for c in range(chunks)
        ]
        passes = [
            remote(relay.at[1, at(c)], arrived.at[at(c)], inner_pass, row_recv, c, {"level": beside})
            for c in range(chunks)
        ]

        @pl.when(inner == 0)
        def _():
            for copy in outward:
                copy.start()

        @pl.when(inner == 1)
        def _():
            for copy in inward[:2]:
                copy.start()
    else:
        swaps = [
            remote(given(c), arrived.at[at(c)], own_send, row_recv, c, {"level": other})
            for c in range(chunks)
        ]
        for copy in swaps:
            copy.start()

    left = sketch_ref[which, :, :RANK].astype(F32)
    right = sketch_ref[which, :, RANK:].astype(F32)
    with_kept = jnp.where(upper == 1, right, left).astype(BF16)
    with_arrived = jnp.where(upper == 1, left, right).astype(BF16)
    keep.wait()

    firsts, seconds, thirds = [], [], []

    def relay_on(c):
        @pl.when(inner == 1)
        def _():
            outward[c].wait_recv()
            swaps[c].start()
            if c + 2 < chunks:
                inward[c + 2].start()
            inward[c].wait_recv()
            passes[c].start()

    def compute(c):
        swaps[c].wait_recv()
        for b in range(c * group, (c + 1) * group):
            block = slice(b * RANK, (b + 1) * RANK)
            z = jnp.dot(with_kept, kept[block, :], preferred_element_type=F32)
            z = z + jnp.dot(with_arrived, arrived[block, :], preferred_element_type=F32)
            z_ref[b] = z
            high, low = split(z)
            high, low = high.astype(BF16), low.astype(BF16)
            gram = lax.dot_general(
                jnp.concatenate((high, low, high, low), axis=1),
                jnp.concatenate((high, high, low, low), axis=1),
                (((1,), (1,)), ((), ())), preferred_element_type=F32,
            )
            part[b] = pack(gram)
        copy = remote(
            part.at[pl.ds(c * group + (1 - core) * half, half)], first.at[pl.ds(c * half, half)],
            first_send, first_recv, c, {"sample": mate},
        )
        copy.start()
        firsts.append(copy)

    def add_first(c):
        firsts[c].wait_recv()
        for b in range(half):
            partial[c * half + b] = part[c * group + core * half + b] + first[c * half + b]
        copy = remote(
            partial.at[pl.ds(c * half, half)], second.at[pl.ds(c * half, half)],
            second_send, second_recv, c, {"sample": across},
        )
        copy.start()
        seconds.append(copy)

    def add_second(c):
        seconds[c].wait_recv()
        for b in range(half):
            gram_ref[c * group + core * half + b] = partial[c * half + b] + second[c * half + b]
        copy = remote(
            gram_ref.at[pl.ds(c * group + core * half, half)], third.at[pl.ds(c * half, half)],
            third_send, third_recv, c, {"sample": mate},
        )
        copy.start()
        thirds.append(copy)

    def take_third(c):
        thirds[c].wait_recv()
        for b in range(half):
            gram_ref[c * group + (1 - core) * half + b] = third[c * half + b]

    stages = (compute, add_first, add_second, take_third)
    if relayed:
        stages = (relay_on,) + stages
    for step in range(chunks + len(stages) - 1):
        for depth, stage in enumerate(stages):
            if 0 <= step - depth < chunks:
                stage(step - depth)
    for copy in firsts + seconds + thirds:
        copy.wait_send()
    if relayed:
        for copy in outward:
            copy.wait_send()

        @pl.when(inner == 1)
        def _():
            for copy in swaps + passes:
                copy.wait_send()
    else:
        for copy in swaps:
            copy.wait_send()


def project(rows, sketch, which, distance, group, relayed):
    count, columns = rows.shape[0] // 2, rows.shape[1]
    boxes = count // RANK
    chunks = boxes // group
    square = (PACKED, RANK)
    vmem = pl.BlockSpec(memory_space=pltpu.VMEM)
    half = pltpu.VMEM((boxes // 2,) + square, F32)
    return pl.pallas_call(
        functools.partial(project_kernel, which, distance, group, relayed),
        out_shape=(
            jax.ShapeDtypeStruct((boxes, RANK, columns), F32),
            jax.ShapeDtypeStruct((boxes,) + square, F32),
        ),
        in_specs=[pl.BlockSpec(memory_space=pltpu.HBM), vmem],
        out_specs=(vmem, vmem),
        scratch_shapes=[
            pltpu.VMEM((count, columns), BF16),
            pltpu.VMEM((2, count if relayed else 16, columns), BF16),
            pltpu.VMEM((count, columns), BF16),
            pltpu.VMEM((boxes,) + square, F32),
            half, half, half, half,
            pltpu.SemaphoreType.DMA,
        ] + [pltpu.SemaphoreType.DMA((chunks,))] * 12,
        compiler_params=pltpu.CompilerParams(
            collective_id=which, has_side_effects=True, vmem_limit_bytes=40 * 2**20
        ),
    )(rows, sketch)


def factor_kernel(gram_ref, z_ref, factor_ref, rows_ref, work, done):
    boxes, order = z_ref.shape[:2]
    strip = 4 * PANEL
    lane = lax.broadcasted_iota(jnp.int32, (PANEL, 128), 1)
    row = lax.broadcasted_iota(jnp.int32, (PANEL, 128), 0)
    box_of = lane // PANEL
    unit = (lane % PANEL == row).astype(F32)
    zeros = jnp.zeros((PANEL, 128), F32)
    picks = [box_of * PANEL + k for k in range(PANEL)]
    tiles = range(4)

    for m in range(boxes):
        work[m, :, :order] = unpack(gram_ref[m])
    work[:, :, order:] = z_ref[...]

    def across_rows(value, j):
        return jnp.broadcast_to(value[j:j + 1, :], value.shape)

    def turn(value, groups):
        shift = groups * PANEL % 128
        return pltpu.roll(value, shift, axis=1) if shift else value

    def strip_inverse(top):
        grid = [[unit if a == c else zeros for c in tiles] for a in tiles]
        for a in tiles:
            for m in range(boxes):
                old = work[m, top + a * PANEL:top + (a + 1) * PANEL, :order]
                for c in tiles:
                    moved = turn(old, m - top // PANEL - c)
                    grid[a][c] = jnp.where(box_of == m, moved, grid[a][c])
        for b in tiles:
            rest = range(b, 4)
            column = {
                (a, k): jnp.take_along_axis(grid[a][b], picks[k], axis=1)
                for a in rest for k in range(PANEL)
            }
            for a in rest:
                grid[a][b] = unit if a == b else zeros
            for j in range(PANEL):
                scale = lax.rsqrt(across_rows(column[b, j], j))
                below = {a: column[a, j] * scale for a in rest}
                for k in range(j + 1, PANEL):
                    solved = across_rows(column[b, k], j) * scale
                    for a in rest:
                        column[a, k] = column[a, k] - below[a] * solved
                for c in tiles:
                    solved = across_rows(grid[b][c], j) * scale
                    for a in rest:
                        new = grid[a][c] - below[a] * solved
                        if a == b:
                            new = jnp.where(row > j, new, jnp.where(row == j, solved, grid[a][c]))
                        grid[a][c] = new
        return grid

    for top in range(0, order, strip):
        grid = strip_inverse(top)
        panels = []
        for m in range(boxes):
            pieces = []
            for a in tiles:
                piece = zeros
                for c in range(a + 1):
                    piece = jnp.where(box_of == c, turn(grid[a][c], c - m), piece)
                pieces.append(piece)
            inverse = jnp.concatenate(pieces, axis=0)[:, :strip]
            high, low = split(inverse)
            left = jnp.concatenate((high, low), axis=0).astype(BF16)
            high, low = split(work[m, top:top + strip, :])
            right = jnp.concatenate((high, low), axis=1).astype(BF16)
            terms = jnp.dot(left, right, preferred_element_type=F32)
            wide = terms.shape[1] // 2
            new = terms[:strip, :wide] + (
                terms[strip:, :wide] + terms[:strip, wide:] + terms[strip:, wide:]
            )
            done[m, top:top + strip, :] = new
            panels.append(new)
        if top + strip < order:
            for m in range(boxes):
                high, low = split(panels[m])
                right = jnp.concatenate((high, high, low, low), axis=0).astype(BF16)
                left = jnp.concatenate((high, low, high, low), axis=0)[:, :order]
                left = left.T[top + strip:, :].astype(BF16)
                work[m, top + strip:, :] = work[m, top + strip:, :] - jnp.dot(
                    left, right, preferred_element_type=F32
                )

    keep = lax.broadcasted_iota(jnp.int32, (order, order), 0) >= lax.broadcasted_iota(
        jnp.int32, (order, order), 1
    )
    for m in range(boxes):
        factor_ref[m] = jnp.where(keep, done[m, :, :order].T, 0.0)
        rows_ref[m] = (done[m, :, order:] * math.sqrt(SAMPLES)).astype(rows_ref.dtype)


def factor(gram, z, dtype):
    boxes, order, columns = z.shape
    together = min(16, boxes)
    spec = pl.BlockSpec((together, order, order), lambda i: (i, 0, 0))
    wide = pl.BlockSpec((together, order, columns), lambda i: (i, 0, 0))
    factors, rows = pl.pallas_call(
        factor_kernel,
        grid=(boxes // together,),
        out_shape=(
            jax.ShapeDtypeStruct((boxes, order, order), F32),
            jax.ShapeDtypeStruct((boxes, order, columns), dtype),
        ),
        in_specs=[pl.BlockSpec((together,) + gram.shape[1:], lambda i: (i, 0, 0)), wide],
        out_specs=(spec, wide),
        scratch_shapes=[pltpu.VMEM((together, order, order + columns), F32)] * 2,
        compiler_params=pltpu.CompilerParams(vmem_limit_bytes=40 * 2**20),
    )(gram, z)
    return factors, rows.reshape(boxes * order, columns)


def shards(samples, sketch):
    far = lax.axis_size("level") // 2
    z, gram = project(samples, sketch, 0, far, 2, far >= 2)
    far_factors, first_rows = factor(gram, z, BF16)
    z, gram = project(first_rows, sketch, 1, 1, 2, False)
    near_factors, basis_rows = factor(gram, z, F32)
    return (far_factors, near_factors, basis_rows)


def solution(mesh):
    return jax.shard_map(
        shards,
        mesh=mesh,
        in_specs=(P("level", "sample"), P()),
        out_specs=(P("level", None, None), P("level", None, None), P("level", "sample")),
        check_vma=False,
    )
```

```python
import functools
import math

import jax
import jax.numpy as jnp
from jax import lax
from jax.experimental import pallas as pl
from jax.experimental.pallas import tpu as pltpu
from jax.sharding import PartitionSpec as P

SAMPLES = 512
RANK = 128
PANEL = 8
PACKED = 72
F32 = jnp.float32
BF16 = jnp.bfloat16


def split(value):
    high = value.astype(BF16).astype(F32)
    return high, value - high


def pack_masks():
    side = RANK // 2
    lane = lax.broadcasted_iota(jnp.int32, (side, RANK), 1)
    row = lax.broadcasted_iota(jnp.int32, (side, RANK), 0)
    return lane < side, row - lane % side


def pack(gram):
    side = RANK // 2
    first, below = pack_masks()
    top, bottom = gram[:side, :], gram[side:, :]
    main = jnp.where(first == (below >= 0), top, bottom)
    middle = jnp.where(below == 0, jnp.where(first, bottom, top), 0.0)
    middle = jnp.sum(middle, axis=0, keepdims=True)
    return jnp.concatenate((main, jnp.broadcast_to(middle, (PACKED - side, RANK))), axis=0)


def unpack(packed):
    side = RANK // 2
    first, below = pack_masks()
    main = packed[:side, :]
    middle = jnp.broadcast_to(packed[side:side + 1, :], main.shape)
    turned = jnp.concatenate((main, main), axis=0).T
    lower = jnp.where(below == 0, middle, turned[:side, :])
    upper = jnp.where(below == 0, middle, turned[side:, :])
    top = jnp.where(first, jnp.where(below >= 0, main, turned[:side, :]), jnp.where(below < 0, main, lower))
    bottom = jnp.where(first, jnp.where(below < 0, main, upper), jnp.where(below >= 0, main, turned[side:, :]))
    return jnp.concatenate((top, bottom), axis=0)


def project_kernel(
    which, distance, group, relayed, rows_ref, sketch_ref, z_ref, gram_ref,
    kept, relay, arrived, part, first, partial, second, third, kept_sem,
    own_send, row_recv, outer_recv, inner_recv, outer_pass, inner_pass,
    first_send, first_recv, second_send, second_recv, third_send, third_recv,
):
    level, sample = lax.axis_index("level"), lax.axis_index("sample")
    upper = level // distance % 2
    other = level + distance - 2 * distance * upper
    core = sample % 2
    mate = sample + 1 - 2 * core
    across = sample + 2 - 4 * (sample // 2 % 2)
    count = arrived.shape[0]
    boxes = count // RANK
    chunks = boxes // group
    half = group // 2
    size = group * RANK
    ahead = min(4, chunks)
    if relayed:
        hop = distance // 2
        place = level // hop % 4
        inner = (place + 1) // 2 % 2
        beside = level + hop * (1 - 2 * (place % 2))
        cross = level + hop * (3 - 2 * place)
        targets = ({"level": beside}, {"level": cross}, {"sample": mate}, {"sample": across})
    else:
        targets = ({"level": other}, {"sample": mate}, {"sample": across})

    keep = pltpu.make_async_copy(
        rows_ref.at[pl.ds(pl.multiple_of(upper * count, size), count)], kept, kept_sem
    )
    keep.start()
    barrier = pltpu.get_barrier_semaphore()
    for target in targets:
        pl.semaphore_signal(barrier, inc=1, device_id=target, device_id_type=pl.DeviceIdType.MESH)
    pl.semaphore_wait(barrier, len(targets))

    def remote(src, dst, send, recv, c, target):
        return pltpu.make_async_remote_copy(
            src_ref=src, dst_ref=dst, send_sem=send.at[c], recv_sem=recv.at[c],
            device_id=target, device_id_type=pl.DeviceIdType.MESH,
        )

    def given(c):
        return rows_ref.at[pl.ds(pl.multiple_of((1 - upper) * count + c * size, size), size)]

    def at(c):
        return pl.ds(c * size, size)

    if relayed:
        outward = [
            remote(given(c), relay.at[0, at(c)], own_send, outer_recv, c, {"level": beside})
            for c in range(chunks)
        ]
        inward = [
            remote(given(c), relay.at[1, at(c)], own_send, inner_recv, c, {"level": cross})
            for c in range(chunks)
        ]
        swaps = [
            remote(relay.at[0, at(c)], arrived.at[at(c)], outer_pass, row_recv, c, {"level": cross})
            for c in range(chunks)
        ]
        passes = [
            remote(relay.at[1, at(c)], arrived.at[at(c)], inner_pass, row_recv, c, {"level": beside})
            for c in range(chunks)
        ]

        @pl.when(inner == 0)
        def _():
            for copy in outward:
                copy.start()

        @pl.when(inner == 1)
        def _():
            for copy in inward[:ahead]:
                copy.start()
    else:
        swaps = [
            remote(given(c), arrived.at[at(c)], own_send, row_recv, c, {"level": other})
            for c in range(chunks)
        ]
        for copy in swaps:
            copy.start()

    left = sketch_ref[which, :, :RANK].astype(F32)
    right = sketch_ref[which, :, RANK:].astype(F32)
    with_kept = jnp.where(upper == 1, right, left).astype(BF16)
    with_arrived = jnp.where(upper == 1, left, right).astype(BF16)
    keep.wait()

    firsts, seconds, thirds = [], [], []

    def relay_on(c):
        @pl.when(inner == 1)
        def _():
            outward[c].wait_recv()
            swaps[c].start()
            if c + ahead < chunks:
                inward[c + ahead].start()
            inward[c].wait_recv()
            passes[c].start()

    def compute(c):
        swaps[c].wait_recv()
        for b in range(c * group, (c + 1) * group):
            block = slice(b * RANK, (b + 1) * RANK)
            z = jnp.dot(with_kept, kept[block, :], preferred_element_type=F32)
            z = z + jnp.dot(with_arrived, arrived[block, :], preferred_element_type=F32)
            z_ref[b] = z
            high, low = split(z)
            high, low = high.astype(BF16), low.astype(BF16)
            gram = lax.dot_general(
                jnp.concatenate((high, low, high, low), axis=1),
                jnp.concatenate((high, high, low, low), axis=1),
                (((1,), (1,)), ((), ())), preferred_element_type=F32,
            )
            part[b] = pack(gram)
        copy = remote(
            part.at[pl.ds(c * group + (1 - core) * half, half)], first.at[pl.ds(c * half, half)],
            first_send, first_recv, c, {"sample": mate},
        )
        copy.start()
        firsts.append(copy)

    def add_first(c):
        firsts[c].wait_recv()
        for b in range(half):
            partial[c * half + b] = part[c * group + core * half + b] + first[c * half + b]
        copy = remote(
            partial.at[pl.ds(c * half, half)], second.at[pl.ds(c * half, half)],
            second_send, second_recv, c, {"sample": across},
        )
        copy.start()
        seconds.append(copy)

    def add_second(c):
        seconds[c].wait_recv()
        for b in range(half):
            gram_ref[c * group + core * half + b] = partial[c * half + b] + second[c * half + b]
        copy = remote(
            gram_ref.at[pl.ds(c * group + core * half, half)], third.at[pl.ds(c * half, half)],
            third_send, third_recv, c, {"sample": mate},
        )
        copy.start()
        thirds.append(copy)

    def take_third(c):
        thirds[c].wait_recv()
        for b in range(half):
            gram_ref[c * group + (1 - core) * half + b] = third[c * half + b]

    stages = [(0, compute), (1, add_first), (2, add_second), (3, take_third)]
    if relayed:
        stages = [(0, relay_on)] + [(depth + ahead - 1, stage) for depth, stage in stages]
    for step in range(chunks + stages[-1][0]):
        for depth, stage in stages:
            if 0 <= step - depth < chunks:
                stage(step - depth)
    for copy in firsts + seconds + thirds:
        copy.wait_send()
    if relayed:
        for copy in outward:
            copy.wait_send()

        @pl.when(inner == 1)
        def _():
            for copy in swaps + passes:
                copy.wait_send()
    else:
        for copy in swaps:
            copy.wait_send()


def project(rows, sketch, which, distance, group, relayed):
    count, columns = rows.shape[0] // 2, rows.shape[1]
    boxes = count // RANK
    chunks = boxes // group
    square = (PACKED, RANK)
    vmem = pl.BlockSpec(memory_space=pltpu.VMEM)
    half = pltpu.VMEM((boxes // 2,) + square, F32)
    return pl.pallas_call(
        functools.partial(project_kernel, which, distance, group, relayed),
        out_shape=(
            jax.ShapeDtypeStruct((boxes, RANK, columns), F32),
            jax.ShapeDtypeStruct((boxes,) + square, F32),
        ),
        in_specs=[pl.BlockSpec(memory_space=pltpu.HBM), vmem],
        out_specs=(vmem, vmem),
        scratch_shapes=[
            pltpu.VMEM((count, columns), BF16),
            pltpu.VMEM((2, count if relayed else 16, columns), BF16),
            pltpu.VMEM((count, columns), BF16),
            pltpu.VMEM((boxes,) + square, F32),
            half, half, half, half,
            pltpu.SemaphoreType.DMA,
        ] + [pltpu.SemaphoreType.DMA((chunks,))] * 12,
        compiler_params=pltpu.CompilerParams(
            collective_id=which, has_side_effects=True, vmem_limit_bytes=40 * 2**20
        ),
    )(rows, sketch)


def factor_kernel(gram_ref, z_ref, factor_ref, rows_ref, work, done):
    boxes, order = z_ref.shape[:2]
    strip = 4 * PANEL
    lane = lax.broadcasted_iota(jnp.int32, (PANEL, 128), 1)
    row = lax.broadcasted_iota(jnp.int32, (PANEL, 128), 0)
    box_of = lane // PANEL
    unit = (lane % PANEL == row).astype(F32)
    zeros = jnp.zeros((PANEL, 128), F32)
    picks = [box_of * PANEL + k for k in range(PANEL)]
    tiles = range(4)

    for m in range(boxes):
        work[m, :, :order] = unpack(gram_ref[m])
    work[:, :, order:] = z_ref[...]

    def across_rows(value, j):
        return jnp.broadcast_to(value[j:j + 1, :], value.shape)

    def turn(value, groups):
        shift = groups * PANEL % 128
        return pltpu.roll(value, shift, axis=1) if shift else value

    def strip_inverse(top):
        grid = [[unit if a == c else zeros for c in tiles] for a in tiles]
        for a in tiles:
            for m in range(boxes):
                old = work[m, top + a * PANEL:top + (a + 1) * PANEL, :order]
                for c in tiles:
                    moved = turn(old, m - top // PANEL - c)
                    grid[a][c] = jnp.where(box_of == m, moved, grid[a][c])
        for b in tiles:
            rest = range(b, 4)
            column = {
                (a, k): jnp.take_along_axis(grid[a][b], picks[k], axis=1)
                for a in rest for k in range(PANEL)
            }
            for a in rest:
                grid[a][b] = unit if a == b else zeros
            pivot = across_rows(column[b, 0], 0)
            for j in range(PANEL):
                scale = lax.rsqrt(pivot)
                if j + 1 < PANEL:
                    pivot = across_rows(column[b, j + 1], j + 1) - (
                        across_rows(column[b, j], j + 1) * scale
                    ) * (across_rows(column[b, j + 1], j) * scale)
                below = {a: column[a, j] * scale for a in rest}
                for k in range(j + 1, PANEL):
                    solved = across_rows(column[b, k], j) * scale
                    for a in rest:
                        column[a, k] = column[a, k] - below[a] * solved
                for c in tiles:
                    solved = across_rows(grid[b][c], j) * scale
                    for a in rest:
                        new = grid[a][c] - below[a] * solved
                        if a == b:
                            new = jnp.where(row > j, new, jnp.where(row == j, solved, grid[a][c]))
                        grid[a][c] = new
        return grid

    for top in range(0, order, strip):
        grid = strip_inverse(top)
        panels = []
        for m in range(boxes):
            pieces = []
            for a in tiles:
                piece = zeros
                for c in range(a + 1):
                    piece = jnp.where(box_of == c, turn(grid[a][c], c - m), piece)
                pieces.append(piece)
            inverse = jnp.concatenate(pieces, axis=0)[:, :strip]
            high, low = split(inverse)
            left = jnp.concatenate((high, low), axis=0).astype(BF16)
            high, low = split(work[m, top:top + strip, :])
            right = jnp.concatenate((high, low), axis=1).astype(BF16)
            terms = jnp.dot(left, right, preferred_element_type=F32)
            wide = terms.shape[1] // 2
            new = terms[:strip, :wide] + (
                terms[strip:, :wide] + terms[:strip, wide:] + terms[strip:, wide:]
            )
            done[m, top:top + strip, :] = new
            panels.append(new)
        if top + strip < order:
            for m in range(boxes):
                high, low = split(panels[m])
                right = jnp.concatenate((high, high, low, low), axis=0).astype(BF16)
                left = jnp.concatenate((high, low, high, low), axis=0)[:, :order]
                left = left.T[top + strip:, :].astype(BF16)
                work[m, top + strip:, :] = work[m, top + strip:, :] - jnp.dot(
                    left, right, preferred_element_type=F32
                )

    keep = lax.broadcasted_iota(jnp.int32, (order, order), 0) >= lax.broadcasted_iota(
        jnp.int32, (order, order), 1
    )
    for m in range(boxes):
        factor_ref[m] = jnp.where(keep, done[m, :, :order].T, 0.0)
        rows_ref[m] = (done[m, :, order:] * math.sqrt(SAMPLES)).astype(rows_ref.dtype)


def factor(gram, z, dtype):
    boxes, order, columns = z.shape
    together = min(16, boxes)
    spec = pl.BlockSpec((together, order, order), lambda i: (i, 0, 0))
    wide = pl.BlockSpec((together, order, columns), lambda i: (i, 0, 0))
    factors, rows = pl.pallas_call(
        factor_kernel,
        grid=(boxes // together,),
        out_shape=(
            jax.ShapeDtypeStruct((boxes, order, order), F32),
            jax.ShapeDtypeStruct((boxes, order, columns), dtype),
        ),
        in_specs=[pl.BlockSpec((together,) + gram.shape[1:], lambda i: (i, 0, 0)), wide],
        out_specs=(spec, wide),
        scratch_shapes=[pltpu.VMEM((together, order, order + columns), F32)] * 2,
        compiler_params=pltpu.CompilerParams(vmem_limit_bytes=40 * 2**20),
    )(gram, z)
    return factors, rows.reshape(boxes * order, columns)


def shards(samples, sketch):
    far = lax.axis_size("level") // 2
    z, gram = project(samples, sketch, 0, far, 2, far >= 2)
    far_factors, first_rows = factor(gram, z, BF16)
    z, gram = project(first_rows, sketch, 1, 1, 2, False)
    near_factors, basis_rows = factor(gram, z, F32)
    return (far_factors, near_factors, basis_rows)


def solution(mesh):
    return jax.shard_map(
        shards,
        mesh=mesh,
        in_specs=(P("level", "sample"), P()),
        out_specs=(P("level", None, None), P("level", None, None), P("level", "sample")),
        check_vma=False,
    )
```

```python
import functools
import math

import jax
import jax.numpy as jnp
from jax import lax
from jax.experimental import pallas as pl
from jax.experimental.pallas import tpu as pltpu
from jax.sharding import PartitionSpec as P

SAMPLES = 512
RANK = 128
PANEL = 8
PACKED = 72
F32 = jnp.float32
BF16 = jnp.bfloat16


def split(value):
    high = value.astype(BF16).astype(F32)
    return high, value - high


def pack_masks():
    side = RANK // 2
    lane = lax.broadcasted_iota(jnp.int32, (side, RANK), 1)
    row = lax.broadcasted_iota(jnp.int32, (side, RANK), 0)
    return lane < side, row - lane % side


def pack(gram):
    side = RANK // 2
    first, below = pack_masks()
    top, bottom = gram[:side, :], gram[side:, :]
    main = jnp.where(first == (below >= 0), top, bottom)
    middle = jnp.where(below == 0, jnp.where(first, bottom, top), 0.0)
    middle = jnp.sum(middle, axis=0, keepdims=True)
    return jnp.concatenate((main, jnp.broadcast_to(middle, (PACKED - side, RANK))), axis=0)


def unpack(packed):
    side = RANK // 2
    first, below = pack_masks()
    main = packed[:side, :]
    middle = jnp.broadcast_to(packed[side:side + 1, :], main.shape)
    turned = jnp.concatenate((main, main), axis=0).T
    lower = jnp.where(below == 0, middle, turned[:side, :])
    upper = jnp.where(below == 0, middle, turned[side:, :])
    top = jnp.where(first, jnp.where(below >= 0, main, turned[:side, :]), jnp.where(below < 0, main, lower))
    bottom = jnp.where(first, jnp.where(below < 0, main, upper), jnp.where(below >= 0, main, turned[side:, :]))
    return jnp.concatenate((top, bottom), axis=0)


def project_kernel(
    which, distance, group, relayed, rows_ref, sketch_ref, z_ref, gram_ref,
    kept, relay, arrived, part, first, partial, second, third, kept_sem,
    own_send, row_recv, outer_recv, inner_recv, outer_pass, inner_pass,
    first_send, first_recv, second_send, second_recv, third_send, third_recv,
):
    level, sample = lax.axis_index("level"), lax.axis_index("sample")
    upper = level // distance % 2
    other = level + distance - 2 * distance * upper
    core = sample % 2
    mate = sample + 1 - 2 * core
    across = sample + 2 - 4 * (sample // 2 % 2)
    count = arrived.shape[0]
    boxes = count // RANK
    chunks = boxes // group
    half = group // 2
    size = group * RANK
    ahead = min(3, chunks)
    if relayed:
        hop = distance // 2
        place = level // hop % 4
        inner = (place + 1) // 2 % 2
        beside = level + hop * (1 - 2 * (place % 2))
        cross = level + hop * (3 - 2 * place)
        targets = ({"level": beside}, {"level": cross}, {"sample": mate}, {"sample": across})
    else:
        targets = ({"level": other}, {"sample": mate}, {"sample": across})

    keep = pltpu.make_async_copy(
        rows_ref.at[pl.ds(pl.multiple_of(upper * count, size), count)], kept, kept_sem
    )
    keep.start()
    barrier = pltpu.get_barrier_semaphore()
    for target in targets:
        pl.semaphore_signal(barrier, inc=1, device_id=target, device_id_type=pl.DeviceIdType.MESH)
    pl.semaphore_wait(barrier, len(targets))

    def remote(src, dst, send, recv, c, target):
        return pltpu.make_async_remote_copy(
            src_ref=src, dst_ref=dst, send_sem=send.at[c], recv_sem=recv.at[c],
            device_id=target, device_id_type=pl.DeviceIdType.MESH,
        )

    def given(c):
        return rows_ref.at[pl.ds(pl.multiple_of((1 - upper) * count + c * size, size), size)]

    def at(c):
        return pl.ds(c * size, size)

    if relayed:
        outward = [
            remote(given(c), relay.at[0, at(c)], own_send, outer_recv, c, {"level": beside})
            for c in range(chunks)
        ]
        inward = [
            remote(given(c), relay.at[1, at(c)], own_send, inner_recv, c, {"level": cross})
            for c in range(chunks)
        ]
        swaps = [
            remote(relay.at[0, at(c)], arrived.at[at(c)], outer_pass, row_recv, c, {"level": cross})
            for c in range(chunks)
        ]
        passes = [
            remote(relay.at[1, at(c)], arrived.at[at(c)], inner_pass, row_recv, c, {"level": beside})
            for c in range(chunks)
        ]

        @pl.when(inner == 0)
        def _():
            for copy in outward:
                copy.start()

        @pl.when(inner == 1)
        def _():
            for copy in inward[:ahead]:
                copy.start()
    else:
        swaps = [
            remote(given(c), arrived.at[at(c)], own_send, row_recv, c, {"level": other})
            for c in range(chunks)
        ]
        for copy in swaps[:2]:
            copy.start()

    left = sketch_ref[which, :, :RANK].astype(F32)
    right = sketch_ref[which, :, RANK:].astype(F32)
    with_kept = jnp.where(upper == 1, right, left).astype(BF16)
    with_arrived = jnp.where(upper == 1, left, right).astype(BF16)
    keep.wait()

    firsts, seconds, thirds = [], [], []

    def relay_on(c):
        @pl.when(inner == 1)
        def _():
            outward[c].wait_recv()
            swaps[c].start()
            if c + ahead < chunks:
                inward[c + ahead].start()
            inward[c].wait_recv()
            passes[c].start()

    def compute(c):
        swaps[c].wait_recv()
        if not relayed and c + 2 < chunks:
            swaps[c + 2].start()
        for b in range(c * group, (c + 1) * group):
            block = slice(b * RANK, (b + 1) * RANK)
            z = jnp.dot(with_kept, kept[block, :], preferred_element_type=F32)
            z = z + jnp.dot(with_arrived, arrived[block, :], preferred_element_type=F32)
            z_ref[b] = z
            high, low = split(z)
            high, low = high.astype(BF16), low.astype(BF16)
            gram = lax.dot_general(
                jnp.concatenate((high, low, high, low), axis=1),
                jnp.concatenate((high, high, low, low), axis=1),
                (((1,), (1,)), ((), ())), preferred_element_type=F32,
            )
            part[b] = pack(gram)
        copy = remote(
            part.at[pl.ds(c * group + (1 - core) * half, half)], first.at[pl.ds(c * half, half)],
            first_send, first_recv, c, {"sample": mate},
        )
        copy.start()
        firsts.append(copy)

    def add_first(c):
        firsts[c].wait_recv()
        for b in range(half):
            partial[c * half + b] = part[c * group + core * half + b] + first[c * half + b]
        copy = remote(
            partial.at[pl.ds(c * half, half)], second.at[pl.ds(c * half, half)],
            second_send, second_recv, c, {"sample": across},
        )
        copy.start()
        seconds.append(copy)

    def add_second(c):
        seconds[c].wait_recv()
        for b in range(half):
            gram_ref[c * group + core * half + b] = partial[c * half + b] + second[c * half + b]
        copy = remote(
            gram_ref.at[pl.ds(c * group + core * half, half)], third.at[pl.ds(c * half, half)],
            third_send, third_recv, c, {"sample": mate},
        )
        copy.start()
        thirds.append(copy)

    def take_third(c):
        thirds[c].wait_recv()
        for b in range(half):
            gram_ref[c * group + (1 - core) * half + b] = third[c * half + b]

    stages = [(0, compute), (1, add_first), (2, add_second), (3, take_third)]
    if relayed:
        stages = [(0, relay_on)] + [(depth + 3, stage) for depth, stage in stages]
    for step in range(chunks + stages[-1][0]):
        for depth, stage in stages:
            if 0 <= step - depth < chunks:
                stage(step - depth)
    for copy in firsts + seconds + thirds:
        copy.wait_send()
    if relayed:
        for copy in outward:
            copy.wait_send()

        @pl.when(inner == 1)
        def _():
            for copy in swaps + passes:
                copy.wait_send()
    else:
        for copy in swaps:
            copy.wait_send()


def project(rows, sketch, which, distance, group, relayed):
    count, columns = rows.shape[0] // 2, rows.shape[1]
    boxes = count // RANK
    chunks = boxes // group
    square = (PACKED, RANK)
    vmem = pl.BlockSpec(memory_space=pltpu.VMEM)
    half = pltpu.VMEM((boxes // 2,) + square, F32)
    return pl.pallas_call(
        functools.partial(project_kernel, which, distance, group, relayed),
        out_shape=(
            jax.ShapeDtypeStruct((boxes, RANK, columns), F32),
            jax.ShapeDtypeStruct((boxes,) + square, F32),
        ),
        in_specs=[pl.BlockSpec(memory_space=pltpu.HBM), vmem],
        out_specs=(vmem, vmem),
        scratch_shapes=[
            pltpu.VMEM((count, columns), BF16),
            pltpu.VMEM((2, count if relayed else 16, columns), BF16),
            pltpu.VMEM((count, columns), BF16),
            pltpu.VMEM((boxes,) + square, F32),
            half, half, half, half,
            pltpu.SemaphoreType.DMA,
        ] + [pltpu.SemaphoreType.DMA((chunks,))] * 12,
        compiler_params=pltpu.CompilerParams(
            collective_id=which, has_side_effects=True, vmem_limit_bytes=40 * 2**20
        ),
    )(rows, sketch)


def factor_kernel(gram_ref, z_ref, factor_ref, rows_ref, work, done):
    boxes, order = z_ref.shape[:2]
    strip = 4 * PANEL
    lane = lax.broadcasted_iota(jnp.int32, (PANEL, 128), 1)
    row = lax.broadcasted_iota(jnp.int32, (PANEL, 128), 0)
    box_of = lane // PANEL
    unit = (lane % PANEL == row).astype(F32)
    zeros = jnp.zeros((PANEL, 128), F32)
    picks = [box_of * PANEL + k for k in range(PANEL)]
    tiles = range(4)

    for m in range(boxes):
        work[m, :, :order] = unpack(gram_ref[m])
    work[:, :, order:] = z_ref[...]

    def across_rows(value, j):
        return jnp.broadcast_to(value[j:j + 1, :], value.shape)

    def turn(value, groups):
        shift = groups * PANEL % 128
        return pltpu.roll(value, shift, axis=1) if shift else value

    def strip_inverse(top):
        grid = [[unit if a == c else zeros for c in tiles] for a in tiles]
        for a in tiles:
            for m in range(boxes):
                old = work[m, top + a * PANEL:top + (a + 1) * PANEL, :order]
                for c in tiles:
                    moved = turn(old, m - top // PANEL - c)
                    grid[a][c] = jnp.where(box_of == m, moved, grid[a][c])
        for b in tiles:
            rest = range(b, 4)
            column = {
                (a, k): jnp.take_along_axis(grid[a][b], picks[k], axis=1)
                for a in rest for k in range(PANEL)
            }
            for a in rest:
                grid[a][b] = unit if a == b else zeros
            pivot = across_rows(column[b, 0], 0)
            for j in range(PANEL):
                scale = lax.rsqrt(pivot)
                if j + 1 < PANEL:
                    pivot = across_rows(column[b, j + 1], j + 1) - (
                        across_rows(column[b, j], j + 1) * scale
                    ) * (across_rows(column[b, j + 1], j) * scale)
                below = {a: column[a, j] * scale for a in rest}
                for k in range(j + 1, PANEL):
                    solved = across_rows(column[b, k], j) * scale
                    for a in rest:
                        column[a, k] = column[a, k] - below[a] * solved
                for c in tiles:
                    solved = across_rows(grid[b][c], j) * scale
                    for a in rest:
                        new = grid[a][c] - below[a] * solved
                        if a == b:
                            new = jnp.where(row > j, new, jnp.where(row == j, solved, grid[a][c]))
                        grid[a][c] = new
        return grid

    for top in range(0, order, strip):
        grid = strip_inverse(top)
        panels = []
        for m in range(boxes):
            pieces = []
            for a in tiles:
                piece = zeros
                for c in range(a + 1):
                    piece = jnp.where(box_of == c, turn(grid[a][c], c - m), piece)
                pieces.append(piece)
            inverse = jnp.concatenate(pieces, axis=0)[:, :strip]
            high, low = split(inverse)
            left = jnp.concatenate((high, low), axis=0).astype(BF16)
            high, low = split(work[m, top:top + strip, :])
            right = jnp.concatenate((high, low), axis=1).astype(BF16)
            terms = jnp.dot(left, right, preferred_element_type=F32)
            wide = terms.shape[1] // 2
            new = terms[:strip, :wide] + (
                terms[strip:, :wide] + terms[:strip, wide:] + terms[strip:, wide:]
            )
            done[m, top:top + strip, :] = new
            panels.append(new)
        if top + strip < order:
            for m in range(boxes):
                high, low = split(panels[m])
                right = jnp.concatenate((high, high, low, low), axis=0).astype(BF16)
                left = jnp.concatenate((high, low, high, low), axis=0)[:, :order]
                left = left.T[top + strip:, :].astype(BF16)
                work[m, top + strip:, :] = work[m, top + strip:, :] - jnp.dot(
                    left, right, preferred_element_type=F32
                )

    keep = lax.broadcasted_iota(jnp.int32, (order, order), 0) >= lax.broadcasted_iota(
        jnp.int32, (order, order), 1
    )
    for m in range(boxes):
        factor_ref[m] = jnp.where(keep, done[m, :, :order].T, 0.0)
        rows_ref[m] = (done[m, :, order:] * math.sqrt(SAMPLES)).astype(rows_ref.dtype)


def factor(gram, z, dtype):
    boxes, order, columns = z.shape
    together = min(16, boxes)
    spec = pl.BlockSpec((together, order, order), lambda i: (i, 0, 0))
    wide = pl.BlockSpec((together, order, columns), lambda i: (i, 0, 0))
    factors, rows = pl.pallas_call(
        factor_kernel,
        grid=(boxes // together,),
        out_shape=(
            jax.ShapeDtypeStruct((boxes, order, order), F32),
            jax.ShapeDtypeStruct((boxes, order, columns), dtype),
        ),
        in_specs=[pl.BlockSpec((together,) + gram.shape[1:], lambda i: (i, 0, 0)), wide],
        out_specs=(spec, wide),
        scratch_shapes=[pltpu.VMEM((together, order, order + columns), F32)] * 2,
        compiler_params=pltpu.CompilerParams(vmem_limit_bytes=40 * 2**20),
    )(gram, z)
    return factors, rows.reshape(boxes * order, columns)


def shards(samples, sketch):
    far = lax.axis_size("level") // 2
    z, gram = project(samples, sketch, 0, far, 2, far >= 2)
    far_factors, first_rows = factor(gram, z, BF16)
    z, gram = project(first_rows, sketch, 1, 1, 2, False)
    near_factors, basis_rows = factor(gram, z, F32)
    return (far_factors, near_factors, basis_rows)


def solution(mesh):
    return jax.shard_map(
        shards,
        mesh=mesh,
        in_specs=(P("level", "sample"), P()),
        out_specs=(P("level", None, None), P("level", None, None), P("level", "sample")),
        check_vma=False,
    )
```
